256 devices in a mesh: section: 16 (over x_hi, y, core), dp: 16 (over z, x_lo).
Axes of the slice: x: 4 (x_hi: 2, x_lo: 2; x = x_hi * 2 + x_lo), y: 4, z: 8, core: 2. Of those that a mesh axis runs over, the one named last changes fastest.
Arguments:
- tokens: bfloat16 [16, 4, 32, 6144], P('dp'), may hold values from -6 to 6
- segments: int32 [16, 4, 32], P('dp'), may hold values from 0 to 7, never falling along the last dimension, each value on 1 to 16 neighbouring positions
- counts: int32 [16, 4], P('dp'), may hold values from 1 to 32
- down_weights: bfloat16 [16, 6144, 384], P('section')
- up_weights: bfloat16 [16, 6144, 384], P('section')
Outputs:
- section_grads: float32 [16, 6144, 384], P('section', 'dp')
The draws below stay inside these ranges and needn't reach their ends.
All inputs are finite; a program needn't handle non-finite values.
Results may differ from the reference program's by a relative error of at most 0.03.
Values may be sent and summed in bfloat16 or wider, within the bound.
No kernel may reach another device: no remote copies, remote signals or barrier semaphores. Data moves between devices by JAX's collectives and lax.ppermute only.
A program may use at most 128 MiB of HBM per device.

```python
import math
import jax
import jax.numpy as jnp
import numpy as np
from jax import lax

D = 6144
HEAD = 96
SEQ = 32
MICRO = 2
SECTIONS = 16
REPLICAS = 16


def scale_columns(base):
    columns = jnp.arange(4 * HEAD)
    scale = jnp.where(columns < 3 * HEAD, float(D) ** (-0.5), float(HEAD) ** (-0.5)).astype(jnp.float32)
    return (base * scale).astype(jnp.bfloat16)


def draw_down_weights(key, part):
    key = jax.random.fold_in(key, 11)
    shape = (SECTIONS, D, 4 * HEAD)
    base = jax.random.normal(key, shape, jnp.float32)
    return scale_columns(base)


def draw_up_weights(key, part):
    key = jax.random.fold_in(key, 12)
    shape = (SECTIONS, D, 4 * HEAD)
    base = jax.random.normal(key, shape, jnp.float32)
    return scale_columns(base)


def place_ends(entries, key, least, largest):
    longest = entries.shape.index(max(entries.shape))
    spots = []
    for shift in (0, 1):
        where = [jax.random.randint(jax.random.fold_in(key, axis), (), 0, length) for axis, length in enumerate(entries.shape)]
        where[longest] = (where[longest] + shift) % entries.shape[longest]
        spots.append(tuple(where))
    return entries.at[spots[0]].set(least).at[spots[1]].set(largest)


def levels(key, extent, split, least, top_value):
    gain = 1.0
    for position, shards_of in split:
        draws = jax.random.uniform(jax.random.fold_in(jax.random.fold_in(key, 6), position), (shards_of,), jnp.float32, least / len(split), top_value / len(split))
        gain = gain * jnp.repeat(jnp.exp(draws), extent[position] // shards_of).reshape((-1,) + (1,) * (len(extent) - 1 - position))
    return gain


def split_up(amount, total, most, skew):
    loads = [(1 << 20) // math.isqrt(grade ** skew) + 1 for grade in range(2, amount + 1)]
    surplus, holding = total - most - (amount - 1), [1] * (amount - 1)
    while surplus > 0:
        movable = [i for i in range(amount - 1) if holding[i] < most]
        mass, left = sum([loads[i] for i in movable]), surplus
        for i in movable:
            addition = min(most - holding[i], max(1, left * loads[i] // mass), surplus)
            holding[i] = holding[i] + addition
            surplus = surplus - addition
    return np.array([most] + holding)


def uneven_parts(stream_key, count, total, bound, skew):
    if count == 2:
        one = jax.random.randint(stream_key, (), max(1, total - bound), min(bound, total - 1) + 1)
        return jnp.stack([one, total - one])
    tallies = jnp.asarray(split_up(count, total, bound, skew), jnp.int32)
    couples = (count - 1) // 2
    giver, sink = tallies[1:1 + 2 * couples:2], tallies[2:2 + 2 * couples:2]
    slack = jnp.minimum(giver - 1, bound - sink)
    passed = jax.random.randint(jax.random.fold_in(stream_key, 1), (couples,), 0, 1 << 20) % (slack + 1)
    tallies = tallies.at[1:1 + 2 * couples:2].set(giver - passed).at[2:2 + 2 * couples:2].set(sink + passed)
    return tallies[jax.random.permutation(jax.random.fold_in(stream_key, 2), count)]


def bell_draw(own_key, extent, spread, most, pieces=(), dtype=jnp.bfloat16):
    factor_of = levels(own_key, extent, pieces, -0.22, 0.18) if pieces else 1.0
    entries = jax.random.normal(own_key, extent, jnp.float32) * spread * factor_of
    return jnp.minimum(jnp.maximum(entries, -most), most).astype(dtype)


def setup_inputs(seed: int = 0) -> dict:
    key_list = jax.random.split(jax.random.key(seed), 6)
    return {
        "tokens": bell_draw(key_list[0], (REPLICAS, 2 * MICRO, SEQ, D), 1.0, 6.0, ((0, 16),)),
        "segments": jax.vmap(lambda own: jnp.searchsorted(jnp.cumsum(uneven_parts(own, max(3, SEQ // 4), SEQ, max(3, SEQ // 2), 1)), jnp.arange(SEQ), side="right"))(jax.random.split(key_list[1], REPLICAS * (2 * MICRO))).reshape((REPLICAS, 2 * MICRO, SEQ)).astype(jnp.int32),
        "counts": place_ends(jax.random.randint(key_list[2], (REPLICAS, 2 * MICRO), 1, SEQ + 1), jax.random.fold_in(key_list[2], 1), 1, SEQ).astype(jnp.int32),
        "down_weights": draw_down_weights(jax.random.fold_in(key_list[5], 71), 0),
        "up_weights": draw_up_weights(jax.random.fold_in(key_list[5], 71), 0),
    }


EPS = 1e-05
NEG = -1e+30

def attend(qkv, doc, head_index):
    seq = qkv.shape[1]
    query_rows = qkv[..., :head_index].astype(jnp.float32)
    key_rows = qkv[..., head_index:2 * head_index].astype(jnp.float32)
    value_rows = qkv[..., 2 * head_index:].astype(jnp.float32)
    score_matrix = jnp.einsum('tcm,tgm->tcg', query_rows, key_rows) * head_index ** (-0.5)
    places = jnp.arange(seq)
    allowed = (doc[:, :, None] == doc[:, None, :]) & (places[None, :, None] >= places[None, None, :])
    score_matrix = jnp.where(allowed, score_matrix, NEG)
    top = lax.optimization_barrier(jnp.max(score_matrix, axis=-1, keepdims=True))
    expo = jnp.exp(score_matrix - top)
    probs_f = expo / lax.optimization_barrier(jnp.sum(expo, axis=-1, keepdims=True))
    probabilities = probs_f.astype(jnp.bfloat16)
    attended_rows = jnp.einsum('rto,rop->rtp', probabilities.astype(jnp.float32), value_rows).astype(jnp.bfloat16)
    return (probs_f, probabilities, attended_rows, query_rows, key_rows, value_rows)

def section_forward(hidden, weight_matrices, doc):
    head_index = weight_matrices.shape[1] // 4
    widened = hidden.astype(jnp.float32)
    inverse = lax.rsqrt(lax.optimization_barrier(jnp.mean(widened * widened, axis=-1, keepdims=True)) + EPS)
    normed = (widened * inverse).astype(jnp.bfloat16)
    widened_weight = weight_matrices.astype(jnp.float32)
    qkv = jnp.einsum('bsd,dc->bsc', normed.astype(jnp.float32), widened_weight[:, :3 * head_index]).astype(jnp.bfloat16)
    probs_f, probabilities, attended_rows, query_rows, key_rows, value_rows = attend(qkv, doc, head_index)
    branch_choice = jnp.einsum('cox,kx->cok', attended_rows.astype(jnp.float32), widened_weight[:, 3 * head_index:])
    return ((widened + branch_choice).astype(jnp.bfloat16), normed, qkv)

def section_backward(hidden, qkv, weight_matrices, doc, output_gradient):
    head_index = weight_matrices.shape[1] // 4
    widened = hidden.astype(jnp.float32)
    inverse = lax.rsqrt(lax.optimization_barrier(jnp.mean(widened * widened, axis=-1, keepdims=True)) + EPS)
    probs_f, probabilities, attended_rows, query_rows, key_rows, value_rows = attend(qkv, doc, head_index)
    widened_weight = weight_matrices.astype(jnp.float32)
    upstream_gradient = output_gradient.astype(jnp.float32)
    attended_gradient = jnp.einsum('eny,yi->eni', upstream_gradient, widened_weight[:, 3 * head_index:])
    probability_gradient = jnp.einsum('tcm,tgm->tcg', attended_gradient, value_rows)
    value_gradient = jnp.einsum('ijv,ijd->ivd', probabilities.astype(jnp.float32), attended_gradient)
    score_gradient = probs_f * (probability_gradient - lax.optimization_barrier(jnp.sum(probs_f * probability_gradient, axis=-1, keepdims=True))) * head_index ** (-0.5)
    query_gradient = jnp.einsum('rto,rop->rtp', score_gradient, key_rows)
    key_gradient = jnp.einsum('ijv,ijd->ivd', score_gradient, query_rows)
    d_project = jnp.concatenate([query_gradient, key_gradient, value_gradient], axis=-1).astype(jnp.bfloat16)
    d_normed = jnp.einsum('bsc,dc->bsd', d_project.astype(jnp.float32), widened_weight[:, :3 * head_index])
    d_hidden = inverse * d_normed - widened * inverse ** 3 * lax.optimization_barrier(jnp.mean(d_normed * widened, axis=-1, keepdims=True))
    grad_in = (upstream_gradient + d_hidden).astype(jnp.bfloat16)
    return (grad_in, d_project, attended_rows)

def reference(tokens, segments, counts, down_weights, up_weights):
    replicas = tokens.shape[0]
    micro = tokens.shape[1] // 2
    seq = tokens.shape[2]
    width = tokens.shape[3]
    total = jnp.sum(counts.astype(jnp.float32))
    loss_weight = counts.astype(jnp.float32) * math.sqrt(2.0 * micro * replicas / seq) / total

    def run(inputs, docs, weight_list, weight_of_loss):
        batch = replicas * micro
        start = inputs.reshape(batch, seq, width)
        doc = docs.reshape(batch, seq)
        hidden = start
        kept = []
        for section in range(SECTIONS):
            output, normed, qkv = section_forward(hidden, weight_list[section], doc)
            kept.append((hidden, normed, qkv))
            hidden = output
        grad = (weight_of_loss.reshape(batch, 1, 1) * (hidden.astype(jnp.float32) - start.astype(jnp.float32))).astype(jnp.bfloat16)
        sums = [None] * SECTIONS
        for section in reversed(range(SECTIONS)):
            saved_in, normed, qkv = kept[section]
            grad_in, d_project, attended_rows = section_backward(saved_in, qkv, weight_list[section], doc, grad)
            shaped = (replicas, micro, seq)
            term_qkv = jnp.einsum('rmsd,rmsc->rdc', normed.reshape(shaped + (width,)).astype(jnp.float32), d_project.reshape(shaped + (d_project.shape[-1],)).astype(jnp.float32))
            term_out = jnp.einsum('rmsd,rmsh->rdh', grad.reshape(shaped + (width,)).astype(jnp.float32), attended_rows.reshape(shaped + (attended_rows.shape[-1],)).astype(jnp.float32))
            terms = jnp.concatenate([term_qkv, term_out], axis=-1).astype(jnp.bfloat16)
            terms = lax.optimization_barrier(terms)
            sums[section] = lax.optimization_barrier(jnp.sum(terms.astype(jnp.float32), axis=0))
            grad = grad_in
        return sums
    down = run(tokens[:, :micro], segments[:, :micro], [down_weights[s] for s in range(SECTIONS)], loss_weight[:, :micro])
    up = run(tokens[:, micro:], segments[:, micro:], [up_weights[SECTIONS - 1 - s] for s in range(SECTIONS)], loss_weight[:, micro:])
    return jnp.stack([down[s] + up[s] for s in range(SECTIONS)])
```

```python
import math

import jax
import jax.numpy as jnp
from jax import lax
from jax.sharding import PartitionSpec as P

EPS = 1e-05
NEG = -1e30
S = 16
R = 16
H = 96
HALF = 8
F32 = jnp.float32
BF16 = jnp.bfloat16


def dot(a, b):
    return lax.dot_general(a, b, (((1,), (0,)), ((), ())), preferred_element_type=F32)


def dot_nt(a, b):
    return lax.dot_general(a, b, (((1,), (1,)), ((), ())), preferred_element_type=F32)


def dot_tn(a, b):
    return lax.dot_general(a, b, (((0,), (0,)), ((), ())), preferred_element_type=F32)


def forward(first, width, docc, docr, nrm, tu, g_low, g_high=None, a_in=None):
    n = docc.shape[0]
    rows = lax.broadcasted_iota(jnp.int32, (n, n), 0)
    cols = lax.broadcasted_iota(jnp.int32, (n, n), 1)
    allowed = (docc == docr) & (rows >= cols)
    if not first:
        early = jnp.concatenate([a_in[k] for k in reversed(range(HALF))], axis=1)
        early = jnp.einsum("tk,skc->stc", early, g_high, preferred_element_type=F32)
    have, keep = [], []
    for i in range(HALF):
        column = i if first else HALF - 1 - i
        acc = tu[column].astype(F32)
        if not first:
            acc = acc + early[column]
        if i > 0:
            past = jnp.concatenate(have if first else have[::-1], axis=1)
            lo, hi = (0, i * H) if first else ((HALF - i) * H, HALF * H)
            acc = acc + dot(past, g_low[column, lo:hi, :])
        gram = g_low[column, column * H : (column + 1) * H, :]
        gram = gram[:, 3 * H :] if first else gram[:, :H]
        out_part = acc[:, 3 * H :]
        rs = lax.rsqrt(jnp.maximum(nrm, 0.0) * (1.0 / width) + EPS)
        qkv = (acc[:, : 3 * H] * rs).astype(BF16)
        q, k_, v = qkv[:, :H], qkv[:, H : 2 * H], qkv[:, 2 * H :]
        score = jnp.where(allowed, dot_nt(q, k_) * H ** (-0.5), NEG)
        expo = jnp.exp(score - jnp.max(score, axis=-1, keepdims=True))
        pf = expo / jnp.sum(expo, axis=-1, keepdims=True)
        a = dot(pf.astype(BF16), v).astype(BF16)
        a_gram = dot(a, gram)
        nrm = nrm + jnp.sum(
            a.astype(F32) * (2.0 * out_part + a_gram), axis=-1, keepdims=True
        )
        have.append(a)
        keep.append((a, qkv, pf, rs, out_part + a_gram))
    return have, keep, nrm


def backward(first, width, lw, tu, g_low, g_high, keep, d=None, gamma=None):
    if not first:
        d = [None] * HALF
        gamma = jnp.zeros_like(lw)
    fulls, gas = [None] * HALF, [None] * HALF
    for i in reversed(range(HALF)):
        column = i if first else HALF - 1 - i
        a, qkv, pf, rs, vg = keep[i]
        a = a.astype(F32)
        u = tu[column][:, 3 * H :].astype(F32)
        w = lw - gamma
        d_here = w * vg - lw * u
        if d[i] is not None:
            d_here = d_here + d[i]
        d_here = d_here.astype(BF16)
        q, k_, v = qkv[:, :H], qkv[:, H : 2 * H], qkv[:, 2 * H :]
        dp = dot_nt(d_here, v)
        dv = dot_tn(pf.astype(BF16), d_here)
        ds = (
            pf * (dp - jnp.sum(pf * dp, axis=-1, keepdims=True)) * H ** (-0.5)
        ).astype(BF16)
        dq = dot(ds, k_)
        dk = dot_tn(ds, q)
        d_project = jnp.concatenate([dq, dk, dv], axis=-1)
        c = rs * rs * (1.0 / width) * jnp.sum(
            d_project * qkv.astype(F32), axis=-1, keepdims=True
        )
        full = jnp.concatenate([rs * d_project, w * a], axis=-1).astype(BF16)
        fulls[i] = full
        gas[i] = (-gamma * a).astype(BF16)
        if i > 0:
            lo, hi = (0, i * H) if first else ((HALF - i) * H, HALF * H)
            part = dot_nt(full, g_low[column, lo:hi, :])
            for k in range(i):
                at = k if first else i - 1 - k
                piece = part[:, at * H : (at + 1) * H]
                d[k] = piece if d[k] is None else d[k] + piece
        gamma = gamma + c
    if first:
        return fulls, gas
    part = jnp.einsum(
        "stc,skc->tk", jnp.stack(fulls[::-1]), g_high, preferred_element_type=F32
    )
    d_mid = [part[:, (HALF - 1 - k) * H : (HALF - k) * H] for k in range(HALF)]
    return fulls, gas, jnp.concatenate(d_mid, axis=1).astype(BF16), gamma


def moved(value, axis, source_of):
    return lax.ppermute(value, axis, [(source_of(i), i) for i in range(lax.axis_size(axis))])


def placed(entries, size):
    result = jnp.zeros((size,) + entries[0][1].shape, entries[0][1].dtype)
    for place, value in entries:
        result = lax.dynamic_update_index_in_dim(result, value, place, 0)
    return result


def ring_z(block, place_of):
    z = lax.axis_index("dp") // 2
    after, before = block, block
    entries = [(place_of(z), block)]
    for step in range(1, 5):
        after = moved(after, "dp", lambda i: (i - 2) % R)
        entries.append((place_of((z - step) % 8), after))
        if step < 4:
            before = moved(before, "dp", lambda i: (i + 2) % R)
            entries.append((place_of((z + step) % 8), before))
    return placed(entries, 8)


def gather_replicas(block):
    x_lo = lax.axis_index("dp") % 2
    other = moved(block, "dp", lambda i: i ^ 1)
    pair = jnp.stack([jnp.where(x_lo == 0, block, other), jnp.where(x_lo == 0, other, block)])
    return ring_z(pair, lambda z: z).reshape((R,) + block.shape)


def turn_y(i, steps):
    return (i & 9) | ((((i >> 1) & 3) + steps) % 4) << 1


def gather_half(block):
    p = lax.axis_index("section")
    parts = [block] + [moved(block, "section", lambda i, a=a: turn_y(i, a)) for a in (1, 2, 3)]
    theirs = [moved(part, "section", lambda i: i ^ 1) for part in parts]
    entries = []
    for steps, (part, their) in enumerate(zip(parts, theirs)):
        source = turn_y(p, steps)
        for device, value in ((source, part), (source ^ 1, their)):
            entries.append((jnp.where(p >= HALF, S - 1 - device, device), value))
    return placed(entries, HALF)


def body(tokens, segments, counts, down_weights, up_weights):
    p = lax.axis_index("section")
    r = lax.axis_index("dp")
    high = p >= HALF
    place = jnp.where(high, S - 1 - p, p)
    x = tokens[0]
    micro = x.shape[0] // 2
    seq = x.shape[1]
    width = x.shape[2]
    rows = width // R
    n = micro * seq
    wd = down_weights[0]
    wu = up_weights[0]

    def ordered(down, up):
        return jnp.where(high, up, down), jnp.where(high, down, up)

    z, x_lo = r // 2, r % 2

    def partner_of(section, replica):
        return ((section // 8) ^ (replica % 2)) * 8 + (replica // 2 - section) % 8

    j = partner_of(p, r)
    down_goes = (p < j) | ((p == j) & ~high)
    wd_o = lax.optimization_barrier(wd[:, 3 * H :])
    wu_o = lax.optimization_barrier(wu[:, 3 * H :])
    send = jnp.where(down_goes, wd_o, wu_o).T
    route = [
        (partner_of(s, q) * R + q, s * R + q) for s in range(S) for q in range(R)
    ]
    got = lax.ppermute(send, ("section", "dp"), route)

    t_first, t_second = ordered(
        dot(x[:micro].reshape(n, width), wd), dot(x[micro:].reshape(n, width), wu)
    )
    x32 = x.astype(F32)
    norms = jnp.sum(x32 * x32, axis=-1).reshape(2 * n, 1)
    diag = (dot_tn(wd_o, wd_o), dot_tn(wu_o, wu_o))
    tu = gather_half(jnp.concatenate([t_first, t_second]).astype(BF16))

    nrm_first, _ = ordered(norms[:n], norms[n:])
    total = jnp.broadcast_to(jnp.sum(counts.astype(F32)), (8, 128))
    for bit in (1, 2, 4, 8):
        total = total + moved(total, "dp", lambda i, bit=bit: i ^ bit)
    total = total[0, 0]
    weights = counts[0].astype(F32) * math.sqrt(2.0 * micro * R / seq) / total
    weights = jnp.broadcast_to(weights[:, None], (2 * micro, seq))
    lw_first, lw_second = ordered(weights[:micro].reshape(n, 1), weights[micro:].reshape(n, 1))
    docs = segments[0] + 16 * jnp.arange(2 * micro)[:, None]
    doc_first, doc_second = ordered(docs[:micro].reshape(n), docs[micro:].reshape(n))

    rows_d = lax.dynamic_slice_in_dim(wd, r * rows, rows, 0)
    rows_u = lax.dynamic_slice_in_dim(wu, r * rows, rows, 0)
    share = x.reshape(2 * micro * seq, width)
    part = 2 * micro * seq // HALF
    share = lax.dynamic_slice_in_dim(share, (p % HALF) * part, part, 0)
    share = share.reshape(part, R, rows).transpose(1, 0, 2)
    share = lax.all_to_all(share, "dp", 0, 0)
    halves = [list(range(HALF)), list(range(HALF, S))]
    x_rows = lax.all_gather(share, "section", axis_index_groups=halves)
    wo_rows = lax.all_gather(
        jnp.concatenate([rows_d[:, 3 * H :].T, rows_u[:, 3 * H :].T]), "section"
    ).reshape(S, 2, H, rows)

    gd, gu = dot(got, wd), dot(got, wu)
    zero = jnp.zeros((H, H), F32)
    mine = jnp.where(high, gu, gd)[:, 3 * H :]
    diagonal = jnp.concatenate([jnp.where(high, diag[0], diag[1]), zero, zero, mine], axis=1)
    block = jnp.where(j < p, gd, jnp.where(j > p, gu, diagonal)).astype(BF16)
    other = moved(block, "dp", lambda i: i ^ 1)

    def slot_of(z_from):
        k = (z_from - p) % 8
        return jnp.where(high, HALF - 1 - k, k)

    g_low = gather_half(ring_z(jnp.where(x_lo == 0, block, other), slot_of).reshape(HALF * H, 4 * H))
    g_high = gather_half(ring_z(jnp.where(x_lo == 0, other, block), slot_of).reshape(HALF * H, 4 * H))
    order = jnp.arange(HALF)

    def cross(value):
        return moved(value, "section", lambda i: i ^ HALF)

    tu_first, tu_second = tu[:, :n], tu[:, n:]
    have1, keep1, nrm1 = forward(
        True, width, doc_first[:, None], doc_first[None, :], nrm_first, tu_first, g_low
    )
    a1 = jnp.stack(have1)
    a_in = cross(a1)
    nrm_in = cross(nrm1)
    have2, keep2, _ = forward(
        False, width, doc_second[:, None], doc_second[None, :], nrm_in, tu_second,
        g_low, g_high, a_in,
    )
    a2 = jnp.stack(have2)
    a_slots = jnp.concatenate(
        [jnp.where((order < place)[:, None, None], a1, a2[::-1]), a_in[::-1]]
    )
    a_slots = a_slots.transpose(1, 0, 2).reshape(n, S * H)
    a_all = gather_replicas(a_slots).reshape(R * n, S * H)
    q2, ga2, d_mid, gamma_mid = backward(
        False, width, lw_second, tu_second, g_low, g_high, keep2
    )
    d_in = cross(d_mid).astype(F32)
    gamma_in = cross(gamma_mid)

    def pick(values, at):
        return lax.dynamic_index_in_dim(jnp.stack(values), at, 0, keepdims=False)

    back = HALF - 1 - place
    second = jnp.concatenate([pick(q2, back), pick(ga2, back), pick(have2, back)], axis=1)
    second = gather_replicas(second).reshape(R * n, 6 * H)
    q1, ga1 = backward(
        True, width, lw_first, tu_first, g_low, None, keep1,
        [d_in[:, k * H : (k + 1) * H] for k in range(HALF)], gamma_in,
    )
    first = jnp.concatenate([pick(q1, place), pick(ga1, place), pick(have1, place)], axis=1)
    first = gather_replicas(first).reshape(R * n, 6 * H)

    x_rows = x_rows.transpose(1, 0, 2, 3).reshape(R, 2, n, rows)
    x_first, x_second = ordered(x_rows[:, 0].reshape(R * n, rows), x_rows[:, 1].reshape(R * n, rows))
    slots = jnp.repeat(jnp.arange(S), H)[:, None]
    b_first = jnp.where(slots < place, dot_tn(a_all, first[:, : 4 * H]), 0.0).astype(BF16)
    b_second = jnp.where(slots > place, dot_tn(a_all, second[:, : 4 * H]), 0.0).astype(BF16)
    wo_rows = jnp.where(high, wo_rows[::-1], wo_rows)
    wo_f = jnp.where(high, wo_rows[:, 1], wo_rows[:, 0]).reshape(S * H, rows)
    wo_s = jnp.where(high, wo_rows[:, 0], wo_rows[:, 1]).reshape(S * H, rows)
    rows_first, rows_second = ordered(rows_d, rows_u)

    def own(x_part, message, wo_part, b_part, rows_part):
        z = jnp.concatenate([message[:, : 3 * H], message[:, 4 * H : 5 * H]], axis=1)
        result = dot_tn(x_part, z) + dot_tn(wo_part, b_part)
        e = dot_tn(message[:, 5 * H :], message[:, 3 * H : 4 * H]).astype(BF16)
        extra = dot(rows_part[:, 3 * H :], e)
        return result + jnp.concatenate([jnp.zeros((rows, 3 * H), F32), extra], axis=1)

    own_first = own(x_first, first, wo_f, b_first, rows_first)
    own_second = own(x_second, second, wo_s, b_second, rows_second)
    keep, away = ordered(own_first, own_second)
    arrived = moved(away.astype(BF16), "section", lambda i: i ^ 15)

    push_first = dot_nt(b_first, rows_first).reshape(S, H, rows)
    push_second = dot_nt(b_second, rows_second).reshape(S, H, rows)
    push = (push_first + push_second[::-1]).astype(BF16)
    push = lax.all_to_all(push, "section", 0, 0)
    push = jnp.sum(push.astype(F32), axis=0).T
    out = keep + arrived.astype(F32)
    out = out + jnp.concatenate([jnp.zeros((rows, 3 * H), F32), push], axis=1)
    return out[None]


def solution(mesh):
    in_specs = (
        P("dp", None, None, None),
        P("dp", None, None),
        P("dp", None),
        P("section", None, None),
        P("section", None, None),
    )
    out_specs = P("section", "dp", None)
    return jax.shard_map(body, mesh=mesh, in_specs=in_specs, out_specs=out_specs, check_vma=False)
```

```python
import math

import jax
import jax.numpy as jnp
from jax import lax
from jax.sharding import PartitionSpec as P

EPS = 1e-05
NEG = -1e30
S = 16
R = 16
H = 96
HALF = 8
F32 = jnp.float32
BF16 = jnp.bfloat16


def dot(a, b):
    return lax.dot_general(a, b, (((1,), (0,)), ((), ())), preferred_element_type=F32)


def dot_nt(a, b):
    return lax.dot_general(a, b, (((1,), (1,)), ((), ())), preferred_element_type=F32)


def dot_tn(a, b):
    return lax.dot_general(a, b, (((0,), (0,)), ((), ())), preferred_element_type=F32)


def forward(first, width, docc, docr, nrm, tu, g_low, g_high=None, a_in=None):
    n = docc.shape[0]
    rows = lax.broadcasted_iota(jnp.int32, (n, n), 0)
    cols = lax.broadcasted_iota(jnp.int32, (n, n), 1)
    allowed = (docc == docr) & (rows >= cols)
    if not first:
        early = jnp.concatenate([a_in[k] for k in reversed(range(HALF))], axis=1)
        early = jnp.einsum("tk,skc->stc", early, g_high, preferred_element_type=F32)
    have, keep = [], []
    for i in range(HALF):
        column = i if first else HALF - 1 - i
        acc = tu[column].astype(F32)
        if not first:
            acc = acc + early[column]
        if i > 0:
            past = jnp.concatenate(have if first else have[::-1], axis=1)
            lo, hi = (0, i * H) if first else ((HALF - i) * H, HALF * H)
            acc = acc + dot(past, g_low[column, lo:hi, :])
        gram = g_low[column, column * H : (column + 1) * H, :]
        gram = gram[:, 3 * H :] if first else gram[:, :H]
        out_part = acc[:, 3 * H :]
        rs = lax.rsqrt(jnp.maximum(nrm, 0.0) * (1.0 / width) + EPS)
        qkv = (acc[:, : 3 * H] * rs).astype(BF16)
        q, k_, v = qkv[:, :H], qkv[:, H : 2 * H], qkv[:, 2 * H :]
        score = jnp.where(allowed, dot_nt(q, k_) * H ** (-0.5), NEG)
        expo = jnp.exp(score - jnp.max(score, axis=-1, keepdims=True))
        pf = expo / jnp.sum(expo, axis=-1, keepdims=True)
        a = dot(pf.astype(BF16), v).astype(BF16)
        a_gram = dot(a, gram)
        nrm = nrm + jnp.sum(
            a.astype(F32) * (2.0 * out_part + a_gram), axis=-1, keepdims=True
        )
        have.append(a)
        keep.append((a, qkv, pf, rs, out_part + a_gram))
    return have, keep, nrm


def backward(first, width, lw, tu, g_low, g_high, keep, d=None, gamma=None, ring=None):
    if not first:
        d = [None] * HALF
        gamma = jnp.zeros_like(lw)
    fulls, gas = [None] * HALF, [None] * HALF
    for i in reversed(range(HALF)):
        column = i if first else HALF - 1 - i
        a, qkv, pf, rs, vg = keep[i]
        a = a.astype(F32)
        u = tu[column][:, 3 * H :].astype(F32)
        w = lw - gamma
        d_here = w * vg - lw * u
        if d[i] is not None:
            d_here = d_here + d[i]
        d_here = d_here.astype(BF16)
        q, k_, v = qkv[:, :H], qkv[:, H : 2 * H], qkv[:, 2 * H :]
        dp = dot_nt(d_here, v)
        dv = dot_tn(pf.astype(BF16), d_here)
        ds = (
            pf * (dp - jnp.sum(pf * dp, axis=-1, keepdims=True)) * H ** (-0.5)
        ).astype(BF16)
        dq = dot(ds, k_)
        dk = dot_tn(ds, q)
        d_project = jnp.concatenate([dq, dk, dv], axis=-1)
        c = rs * rs * (1.0 / width) * jnp.sum(
            d_project * qkv.astype(F32), axis=-1, keepdims=True
        )
        full = jnp.concatenate([rs * d_project, w * a], axis=-1).astype(BF16)
        fulls[i] = full
        gas[i] = (-gamma * a).astype(BF16)
        if i > 0:
            lo, hi = (0, i * H) if first else ((HALF - i) * H, HALF * H)
            part = dot_nt(full, g_low[column, lo:hi, :])
            for k in range(i):
                at = k if first else i - 1 - k
                piece = part[:, at * H : (at + 1) * H]
                d[k] = piece if d[k] is None else d[k] + piece
        gamma = gamma + c
        if i % 2 == 1 or i == 0:
            gamma = ring.advance(gamma)
    if first:
        return fulls, gas
    part = jnp.einsum(
        "stc,skc->tk", jnp.stack(fulls[::-1]), g_high, preferred_element_type=F32
    )
    d_mid = [part[:, (HALF - 1 - k) * H : (HALF - k) * H] for k in range(HALF)]
    return fulls, gas, jnp.concatenate(d_mid, axis=1).astype(BF16), gamma


def moved(value, axis, source_of):
    return lax.ppermute(value, axis, [(source_of(i), i) for i in range(lax.axis_size(axis))])


def placed(entries, size):
    result = jnp.zeros((size,) + entries[0][1].shape, entries[0][1].dtype)
    for place, value in entries:
        result = lax.dynamic_update_index_in_dim(result, value, place, 0)
    return result


def tied(first, *rest):
    return lax.optimization_barrier((first,) + rest)


class Ring:
    def __init__(self, block, place_of):
        self.place_of = place_of
        self.z = lax.axis_index("dp") // 2
        self.after = self.before = block
        self.entries = [(place_of(self.z), block)]
        self.step = 0

    def take(self):
        self.step += 1
        self.after = moved(self.after, "dp", lambda i: (i - 2) % R)
        self.entries.append((self.place_of((self.z - self.step) % 8), self.after))
        if self.step < 4:
            self.before = moved(self.before, "dp", lambda i: (i + 2) % R)
            self.entries.append((self.place_of((self.z + self.step) % 8), self.before))

    def advance(self, value):
        if self.step >= 1:
            value, self.after, self.before = tied(value, self.after, self.before)
        if self.step < 4:
            self.take()
        return value

    def finish(self):
        while self.step < 4:
            self.take()
        return placed(self.entries, 8)


def ring_z(block, place_of):
    return Ring(block, place_of).finish()


def replica_pair(block):
    x_lo = lax.axis_index("dp") % 2
    other = moved(block, "dp", lambda i: i ^ 1)
    return jnp.stack([jnp.where(x_lo == 0, block, other), jnp.where(x_lo == 0, other, block)])


def replica_ring(pair):
    return Ring(pair, lambda z: z)


def turn_y(i, steps):
    return (i & 9) | ((((i >> 1) & 3) + steps) % 4) << 1


def turned(block):
    return [block] + [moved(block, "section", lambda i, a=a: turn_y(i, a)) for a in (1, 2, 3)]


def gather_half(parts):
    p = lax.axis_index("section")
    theirs = [moved(part, "section", lambda i: i ^ 1) for part in parts]
    entries = []
    for steps, (part, their) in enumerate(zip(parts, theirs)):
        source = turn_y(p, steps)
        for device, value in ((source, part), (source ^ 1, their)):
            entries.append((jnp.where(p >= HALF, S - 1 - device, device), value))
    return placed(entries, HALF)


def body(tokens, segments, counts, down_weights, up_weights):
    p = lax.axis_index("section")
    r = lax.axis_index("dp")
    high = p >= HALF
    place = jnp.where(high, S - 1 - p, p)
    x = tokens[0]
    micro = x.shape[0] // 2
    seq = x.shape[1]
    width = x.shape[2]
    rows = width // R
    n = micro * seq
    wd = down_weights[0]
    wu = up_weights[0]

    def ordered(down, up):
        return jnp.where(high, up, down), jnp.where(high, down, up)

    z, x_lo = r // 2, r % 2

    def partner_of(section, replica):
        return ((section // 8) ^ (replica % 2)) * 8 + (replica // 2 - section) % 8

    j = partner_of(p, r)
    down_goes = (p < j) | ((p == j) & ~high)
    chosen = (jnp.arange(H)[:, None] + 3 * H == jnp.arange(4 * H)[None, :]).astype(BF16)
    wd_t = dot_nt(chosen, wd).astype(BF16)
    wu_t = dot_nt(chosen, wu).astype(BF16)
    send = jnp.where(down_goes, wd_t, wu_t)
    route = [
        (partner_of(s, q) * R + q, s * R + q) for s in range(S) for q in range(R)
    ]
    got = lax.ppermute(send, ("section", "dp"), route)
    got, x, counts = tied(got, x, counts)

    t_first, t_second = ordered(
        dot(x[:micro].reshape(n, width), wd), dot(x[micro:].reshape(n, width), wu)
    )
    x32 = x.astype(F32)
    norms = jnp.sum(x32 * x32, axis=-1).reshape(2 * n, 1)
    diag = (dot_nt(wd_t, wd_t), dot_nt(wu_t, wu_t))
    tu = gather_half(turned(jnp.concatenate([t_first, t_second]).astype(BF16)))

    nrm_first, _ = ordered(norms[:n], norms[n:])
    total = jnp.broadcast_to(jnp.sum(counts.astype(F32)), (8, 128))
    for bit in (1, 2, 4, 8):
        total = total + moved(total, "dp", lambda i, bit=bit: i ^ bit)
    total = total[0, 0]
    weights = counts[0].astype(F32) * math.sqrt(2.0 * micro * R / seq) / total
    weights = jnp.broadcast_to(weights[:, None], (2 * micro, seq))
    lw_first, lw_second = ordered(weights[:micro].reshape(n, 1), weights[micro:].reshape(n, 1))
    docs = segments[0] + 16 * jnp.arange(2 * micro)[:, None]
    doc_first, doc_second = ordered(docs[:micro].reshape(n), docs[micro:].reshape(n))

    rows_d = lax.dynamic_slice_in_dim(wd, r * rows, rows, 0)
    rows_u = lax.dynamic_slice_in_dim(wu, r * rows, rows, 0)
    wo_rows = lax.all_gather(
        jnp.concatenate([rows_d[:, 3 * H :].T, rows_u[:, 3 * H :].T]), "section"
    ).reshape(S, 2, H, rows)

    gd, gu = dot(got, wd), dot(got, wu)
    zero = jnp.zeros((H, H), F32)
    mine = jnp.where(high, gu, gd)[:, 3 * H :]
    diagonal = jnp.concatenate([jnp.where(high, diag[0], diag[1]), zero, zero, mine], axis=1)
    block = jnp.where(j < p, gd, jnp.where(j > p, gu, diagonal)).astype(BF16)
    other = moved(block, "dp", lambda i: i ^ 1)

    def slot_of(z_from):
        k = (z_from - p) % 8
        return jnp.where(high, HALF - 1 - k, k)

    low_ring = ring_z(jnp.where(x_lo == 0, block, other), slot_of).reshape(HALF * H, 4 * H)
    high_block, low_ring, x = tied(jnp.where(x_lo == 0, other, block), low_ring, x)
    low_parts = turned(low_ring)
    share = x.reshape(2 * micro * seq, width)
    part = 2 * micro * seq // HALF
    share = lax.dynamic_slice_in_dim(share, (p % HALF) * part, part, 0)
    share = share.reshape(part, R, rows).transpose(1, 0, 2)
    share = lax.all_to_all(share, "dp", 0, 0)
    halves = [list(range(HALF)), list(range(HALF, S))]
    x_rows = lax.all_gather(share, "section", axis_index_groups=halves)
    high_ring = ring_z(high_block, slot_of).reshape(HALF * H, 4 * H)
    low_parts, high_ring = tied(low_parts, high_ring)
    g_low = gather_half(low_parts)
    g_high = gather_half(turned(high_ring))
    order = jnp.arange(HALF)

    def cross(value):
        return moved(value, "section", lambda i: i ^ HALF)

    tu_first, tu_second = tu[:, :n], tu[:, n:]
    have1, keep1, nrm1 = forward(
        True, width, doc_first[:, None], doc_first[None, :], nrm_first, tu_first, g_low
    )
    a1 = jnp.stack(have1)
    a_in = cross(a1)
    nrm_in = cross(nrm1)
    have2, keep2, _ = forward(
        False, width, doc_second[:, None], doc_second[None, :], nrm_in, tu_second,
        g_low, g_high, a_in,
    )
    a2 = jnp.stack(have2)
    a_slots = jnp.concatenate(
        [jnp.where((order < place)[:, None, None], a1, a2[::-1]), a_in[::-1]]
    )
    a_slots = a_slots.transpose(1, 0, 2).reshape(n, S * H)
    a_pair, lw_second = tied(replica_pair(a_slots), lw_second)
    a_ring = replica_ring(a_pair)
    a_ring.take()
    q2, ga2, d_mid, gamma_mid = backward(
        False, width, lw_second, tu_second, g_low, g_high, keep2, ring=a_ring
    )
    a_all = a_ring.finish().reshape(R * n, S * H)
    d_in = cross(d_mid).astype(F32)
    gamma_in = cross(gamma_mid)

    def pick(values, at):
        return lax.dynamic_index_in_dim(jnp.stack(values), at, 0, keepdims=False)

    back = HALF - 1 - place
    second = jnp.concatenate([pick(q2, back), pick(ga2, back), pick(have2, back)], axis=1)
    second_pair, gamma_in = tied(replica_pair(second), gamma_in)
    second_ring = replica_ring(second_pair)
    second_ring.take()
    q1, ga1 = backward(
        True, width, lw_first, tu_first, g_low, None, keep1,
        [d_in[:, k * H : (k + 1) * H] for k in range(HALF)], gamma_in, second_ring,
    )
    second = second_ring.finish().reshape(R * n, 6 * H)
    first = jnp.concatenate([pick(q1, place), pick(ga1, place), pick(have1, place)], axis=1)
    first = replica_ring(replica_pair(first)).finish().reshape(R * n, 6 * H)

    x_rows = x_rows.transpose(1, 0, 2, 3).reshape(R, 2, n, rows)
    x_first, x_second = ordered(x_rows[:, 0].reshape(R * n, rows), x_rows[:, 1].reshape(R * n, rows))
    slots = jnp.repeat(jnp.arange(S), H)[:, None]
    b_first = jnp.where(slots < place, dot_tn(a_all, first[:, : 4 * H]), 0.0).astype(BF16)
    b_second = jnp.where(slots > place, dot_tn(a_all, second[:, : 4 * H]), 0.0).astype(BF16)
    wo_rows = jnp.where(high, wo_rows[::-1], wo_rows)
    wo_f = jnp.where(high, wo_rows[:, 1], wo_rows[:, 0]).reshape(S * H, rows)
    wo_s = jnp.where(high, wo_rows[:, 0], wo_rows[:, 1]).reshape(S * H, rows)
    rows_first, rows_second = ordered(rows_d, rows_u)

    def own(x_part, message, wo_part, b_part, rows_part):
        z = jnp.concatenate([message[:, : 3 * H], message[:, 4 * H : 5 * H]], axis=1)
        result = dot_tn(x_part, z) + dot_tn(wo_part, b_part)
        e = dot_tn(message[:, 5 * H :], message[:, 3 * H : 4 * H]).astype(BF16)
        extra = dot(rows_part[:, 3 * H :], e)
        return result + jnp.concatenate([jnp.zeros((rows, 3 * H), F32), extra], axis=1)

    own_first = own(x_first, first, wo_f, b_first, rows_first)
    own_second = own(x_second, second, wo_s, b_second, rows_second)
    keep, away = ordered(own_first, own_second)
    arrived = moved(away.astype(BF16), "section", lambda i: i ^ 15)

    push_first = dot_nt(b_first, rows_first).reshape(S, H, rows)
    push_second = dot_nt(b_second, rows_second).reshape(S, H, rows)
    push = (push_first + push_second[::-1]).astype(BF16)
    push = lax.all_to_all(push, "section", 0, 0)
    push = jnp.sum(push.astype(F32), axis=0).T
    out = keep + arrived.astype(F32)
    out = out + jnp.concatenate([jnp.zeros((rows, 3 * H), F32), push], axis=1)
    return out[None]


def solution(mesh):
    in_specs = (
        P("dp", None, None, None),
        P("dp", None, None),
        P("dp", None),
        P("section", None, None),
        P("section", None, None),
    )
    out_specs = P("section", "dp", None)
    return jax.shard_map(body, mesh=mesh, in_specs=in_specs, out_specs=out_specs, check_vma=False)
```

```python
import math

import jax
import jax.numpy as jnp
from jax import lax
from jax.sharding import PartitionSpec as P

EPS = 1e-05
NEG = -1e30
S = 16
R = 16
H = 96
HALF = 8
F32 = jnp.float32
BF16 = jnp.bfloat16


def dot(a, b):
    return lax.dot_general(a, b, (((1,), (0,)), ((), ())), preferred_element_type=F32)


def dot_nt(a, b):
    return lax.dot_general(a, b, (((1,), (1,)), ((), ())), preferred_element_type=F32)


def dot_tn(a, b):
    return lax.dot_general(a, b, (((0,), (0,)), ((), ())), preferred_element_type=F32)


def forward(first, width, docc, docr, nrm, tu, g_low, g_high=None, a_in=None):
    n = docc.shape[0]
    rows = lax.broadcasted_iota(jnp.int32, (n, n), 0)
    cols = lax.broadcasted_iota(jnp.int32, (n, n), 1)
    allowed = (docc == docr) & (rows >= cols)
    if not first:
        early = jnp.concatenate([a_in[k] for k in reversed(range(HALF))], axis=1)
        early = jnp.einsum("tk,skc->stc", early, g_high, preferred_element_type=F32)
    have, keep = [], []
    for i in range(HALF):
        column = i if first else HALF - 1 - i
        acc = tu[column].astype(F32)
        if not first:
            acc = acc + early[column]
        if i > 0:
            past = jnp.concatenate(have if first else have[::-1], axis=1)
            lo, hi = (0, i * H) if first else ((HALF - i) * H, HALF * H)
            acc = acc + dot(past, g_low[column, lo:hi, :])
        gram = g_low[column, column * H : (column + 1) * H, :]
        gram = gram[:, 3 * H :] if first else gram[:, :H]
        out_part = acc[:, 3 * H :]
        rs = lax.rsqrt(jnp.maximum(nrm, 0.0) * (1.0 / width) + EPS)
        qkv = (acc[:, : 3 * H] * rs).astype(BF16)
        q, k_, v = qkv[:, :H], qkv[:, H : 2 * H], qkv[:, 2 * H :]
        score = jnp.where(allowed, dot_nt(q, k_) * H ** (-0.5), NEG)
        expo = jnp.exp(score - jnp.max(score, axis=-1, keepdims=True))
        pf = expo / jnp.sum(expo, axis=-1, keepdims=True)
        a = dot(pf.astype(BF16), v).astype(BF16)
        a_gram = dot(a, gram)
        nrm = nrm + jnp.sum(
            a.astype(F32) * (2.0 * out_part + a_gram), axis=-1, keepdims=True
        )
        have.append(a)
        keep.append((a, qkv, pf, rs, out_part + a_gram))
    return have, keep, nrm


def backward(first, width, lw, tu, g_low, g_high, keep, d=None, gamma=None, ring=None):
    if not first:
        d = [None] * HALF
        gamma = jnp.zeros_like(lw)
    fulls, gas = [None] * HALF, [None] * HALF
    for i in reversed(range(HALF)):
        column = i if first else HALF - 1 - i
        a, qkv, pf, rs, vg = keep[i]
        a = a.astype(F32)
        u = tu[column][:, 3 * H :].astype(F32)
        w = lw - gamma
        d_here = w * vg - lw * u
        if d[i] is not None:
            d_here = d_here + d[i]
        d_here = d_here.astype(BF16)
        q, k_, v = qkv[:, :H], qkv[:, H : 2 * H], qkv[:, 2 * H :]
        dp = dot_nt(d_here, v)
        dv = dot_tn(pf.astype(BF16), d_here)
        ds = (
            pf * (dp - jnp.sum(pf * dp, axis=-1, keepdims=True)) * H ** (-0.5)
        ).astype(BF16)
        dq = dot(ds, k_)
        dk = dot_tn(ds, q)
        d_project = jnp.concatenate([dq, dk, dv], axis=-1)
        c = rs * rs * (1.0 / width) * jnp.sum(
            d_project * qkv.astype(F32), axis=-1, keepdims=True
        )
        full = jnp.concatenate([rs * d_project, w * a], axis=-1).astype(BF16)
        fulls[i] = full
        gas[i] = (-gamma * a).astype(BF16)
        if i > 0:
            lo, hi = (0, i * H) if first else ((HALF - i) * H, HALF * H)
            part = dot_nt(full, g_low[column, lo:hi, :])
            for k in range(i):
                at = k if first else i - 1 - k
                piece = part[:, at * H : (at + 1) * H]
                d[k] = piece if d[k] is None else d[k] + piece
        gamma = gamma + c
        if i % 2 == 1 or i == 0:
            gamma = ring.advance(gamma)
    if first:
        return fulls, gas
    part = jnp.einsum(
        "stc,skc->tk", jnp.stack(fulls[::-1]), g_high, preferred_element_type=F32
    )
    d_mid = [part[:, (HALF - 1 - k) * H : (HALF - k) * H] for k in range(HALF)]
    return fulls, gas, jnp.concatenate(d_mid, axis=1).astype(BF16), gamma


def moved(value, axis, source_of):
    return lax.ppermute(value, axis, [(source_of(i), i) for i in range(lax.axis_size(axis))])


def placed(entries, size):
    result = jnp.zeros((size,) + entries[0][1].shape, entries[0][1].dtype)
    for place, value in entries:
        result = lax.dynamic_update_index_in_dim(result, value, place, 0)
    return result


def tied(first, *rest):
    return lax.optimization_barrier((first,) + rest)


class Ring:
    def __init__(self, block, place_of):
        self.place_of = place_of
        self.z = lax.axis_index("dp") // 2
        self.after = self.before = block
        self.entries = [(place_of(self.z), block)]
        self.step = 0

    def take(self):
        self.step += 1
        self.after = moved(self.after, "dp", lambda i: (i - 2) % R)
        self.entries.append((self.place_of((self.z - self.step) % 8), self.after))
        if self.step < 4:
            self.before = moved(self.before, "dp", lambda i: (i + 2) % R)
            self.entries.append((self.place_of((self.z + self.step) % 8), self.before))

    def advance(self, value):
        if self.step >= 1:
            value, self.after, self.before = tied(value, self.after, self.before)
        if self.step < 4:
            self.take()
        return value

    def finish(self):
        while self.step < 4:
            self.take()
        return placed(self.entries, 8)


def ring_z(block, place_of):
    return Ring(block, place_of).finish()


def replica_pair(block):
    x_lo = lax.axis_index("dp") % 2
    other = moved(block, "dp", lambda i: i ^ 1)
    return jnp.stack([jnp.where(x_lo == 0, block, other), jnp.where(x_lo == 0, other, block)])


def replica_ring(pair):
    return Ring(pair, lambda z: z)


def turn_y(i, steps):
    return (i & 9) | ((((i >> 1) & 3) + steps) % 4) << 1


def turned(block):
    return [block] + [moved(block, "section", lambda i, a=a: turn_y(i, a)) for a in (1, 2, 3)]


def gather_half(parts):
    p = lax.axis_index("section")
    theirs = [moved(part, "section", lambda i: i ^ 1) for part in parts]
    entries = []
    for steps, (part, their) in enumerate(zip(parts, theirs)):
        source = turn_y(p, steps)
        for device, value in ((source, part), (source ^ 1, their)):
            entries.append((jnp.where(p >= HALF, S - 1 - device, device), value))
    return placed(entries, HALF)


def body(tokens, segments, counts, down_weights, up_weights):
    p = lax.axis_index("section")
    r = lax.axis_index("dp")
    high = p >= HALF
    place = jnp.where(high, S - 1 - p, p)
    x = tokens[0]
    micro = x.shape[0] // 2
    seq = x.shape[1]
    width = x.shape[2]
    rows = width // R
    n = micro * seq
    wd = down_weights[0]
    wu = up_weights[0]

    def ordered(down, up):
        return jnp.where(high, up, down), jnp.where(high, down, up)

    z, x_lo = r // 2, r % 2

    def partner_of(section, replica):
        return ((section // 8) ^ (replica % 2)) * 8 + (replica // 2 - section) % 8

    j = partner_of(p, r)
    down_goes = (p < j) | ((p == j) & ~high)
    chosen = (jnp.arange(H)[:, None] + 3 * H == jnp.arange(4 * H)[None, :]).astype(BF16)
    wd_t = dot_nt(chosen, wd).astype(BF16)
    wu_t = dot_nt(chosen, wu).astype(BF16)
    send = jnp.where(down_goes, wd_t, wu_t)
    route = [
        (partner_of(s, q) * R + q, s * R + q) for s in range(S) for q in range(R)
    ]
    got = lax.ppermute(send, ("section", "dp"), route)

    rows_d = lax.dynamic_slice_in_dim(wd, r * rows, rows, 0)
    rows_u = lax.dynamic_slice_in_dim(wu, r * rows, rows, 0)
    wo_rows = lax.all_gather(
        jnp.concatenate([rows_d[:, 3 * H :].T, rows_u[:, 3 * H :].T]), "section"
    ).reshape(S, 2, H, rows)

    gd, gu = dot(got, wd), dot(got, wu)
    diag = (dot_nt(wd_t, wd_t), dot_nt(wu_t, wu_t))
    zero = jnp.zeros((H, H), F32)
    mine = jnp.where(high, gu, gd)[:, 3 * H :]
    diagonal = jnp.concatenate([jnp.where(high, diag[0], diag[1]), zero, zero, mine], axis=1)
    block = jnp.where(j < p, gd, jnp.where(j > p, gu, diagonal)).astype(BF16)
    other = moved(block, "dp", lambda i: i ^ 1)
    other, x = tied(other, x)

    t_first, t_second = ordered(
        dot(x[:micro].reshape(n, width), wd), dot(x[micro:].reshape(n, width), wu)
    )
    x32 = x.astype(F32)
    norms = jnp.sum(x32 * x32, axis=-1).reshape(2 * n, 1)
    tu = gather_half(turned(jnp.concatenate([t_first, t_second]).astype(BF16)))

    nrm_first, _ = ordered(norms[:n], norms[n:])
    docs = segments[0] + 16 * jnp.arange(2 * micro)[:, None]
    doc_first, doc_second = ordered(docs[:micro].reshape(n), docs[micro:].reshape(n))

    def slot_of(z_from):
        k = (z_from - p) % 8
        return jnp.where(high, HALF - 1 - k, k)

    low_ring = ring_z(jnp.where(x_lo == 0, block, other), slot_of).reshape(HALF * H, 4 * H)
    high_block, low_ring, x = tied(jnp.where(x_lo == 0, other, block), low_ring, x)
    low_parts = turned(low_ring)
    share = x.reshape(2 * micro * seq, width)
    part = 2 * micro * seq // HALF
    share = lax.dynamic_slice_in_dim(share, (p % HALF) * part, part, 0)
    share = share.reshape(part, R, rows).transpose(1, 0, 2)
    share = lax.all_to_all(share, "dp", 0, 0)
    halves = [list(range(HALF)), list(range(HALF, S))]
    x_rows = lax.all_gather(share, "section", axis_index_groups=halves)
    high_ring = ring_z(high_block, slot_of).reshape(HALF * H, 4 * H)
    low_parts, high_ring = tied(low_parts, high_ring)
    g_low = gather_half(low_parts)
    g_high = gather_half(turned(high_ring))
    order = jnp.arange(HALF)

    def cross(value):
        return moved(value, "section", lambda i: i ^ HALF)

    tu_first, tu_second = tu[:, :n], tu[:, n:]
    have1, keep1, nrm1 = forward(
        True, width, doc_first[:, None], doc_first[None, :], nrm_first, tu_first, g_low
    )
    a1 = jnp.stack(have1)
    a_in = cross(a1)
    nrm_in = cross(nrm1)
    a_in, counts = tied(a_in, counts)
    total = jnp.broadcast_to(jnp.sum(counts.astype(F32)), (8, 128))
    for bit in (1, 2, 4, 8):
        total = total + moved(total, "dp", lambda i, bit=bit: i ^ bit)
    total = total[0, 0]
    weights = counts[0].astype(F32) * math.sqrt(2.0 * micro * R / seq) / total
    weights = jnp.broadcast_to(weights[:, None], (2 * micro, seq))
    lw_first, lw_second = ordered(weights[:micro].reshape(n, 1), weights[micro:].reshape(n, 1))
    have2, keep2, _ = forward(
        False, width, doc_second[:, None], doc_second[None, :], nrm_in, tu_second,
        g_low, g_high, a_in,
    )
    a2 = jnp.stack(have2)
    a_slots = jnp.concatenate(
        [jnp.where((order < place)[:, None, None], a1, a2[::-1]), a_in[::-1]]
    )
    a_slots = a_slots.transpose(1, 0, 2).reshape(n, S * H)
    a_pair, lw_second = tied(replica_pair(a_slots), lw_second)
    a_ring = replica_ring(a_pair)
    a_ring.take()
    q2, ga2, d_mid, gamma_mid = backward(
        False, width, lw_second, tu_second, g_low, g_high, keep2, ring=a_ring
    )
    a_all = a_ring.finish().reshape(R * n, S * H)
    d_in = cross(d_mid).astype(F32)
    gamma_in = cross(gamma_mid)

    def pick(values, at):
        return lax.dynamic_index_in_dim(jnp.stack(values), at, 0, keepdims=False)

    back = HALF - 1 - place
    second = jnp.concatenate([pick(q2, back), pick(ga2, back), pick(have2, back)], axis=1)
    second_pair, gamma_in = tied(replica_pair(second), gamma_in)
    second_ring = replica_ring(second_pair)
    second_ring.take()
    q1, ga1 = backward(
        True, width, lw_first, tu_first, g_low, None, keep1,
        [d_in[:, k * H : (k + 1) * H] for k in range(HALF)], gamma_in, second_ring,
    )
    second = second_ring.finish().reshape(R * n, 6 * H)
    first = jnp.concatenate([pick(q1, place), pick(ga1, place), pick(have1, place)], axis=1)
    first_ring = replica_ring(replica_pair(first))
    first_ring.take()
    x_rows = x_rows.transpose(1, 0, 2, 3).reshape(R, 2, n, rows)
    x_first, x_second = ordered(x_rows[:, 0].reshape(R * n, rows), x_rows[:, 1].reshape(R * n, rows))
    slots = jnp.repeat(jnp.arange(S), H)[:, None]
    b_second = jnp.where(slots > place, dot_tn(a_all, second[:, : 4 * H]), 0.0).astype(BF16)
    wo_rows = jnp.where(high, wo_rows[::-1], wo_rows)
    wo_f = jnp.where(high, wo_rows[:, 1], wo_rows[:, 0]).reshape(S * H, rows)
    wo_s = jnp.where(high, wo_rows[:, 0], wo_rows[:, 1]).reshape(S * H, rows)
    rows_first, rows_second = ordered(rows_d, rows_u)

    def own(x_part, message, wo_part, b_part, rows_part):
        z = jnp.concatenate([message[:, : 3 * H], message[:, 4 * H : 5 * H]], axis=1)
        result = dot_tn(x_part, z) + dot_tn(wo_part, b_part)
        e = dot_tn(message[:, 5 * H :], message[:, 3 * H : 4 * H]).astype(BF16)
        extra = dot(rows_part[:, 3 * H :], e)
        return result + jnp.concatenate([jnp.zeros((rows, 3 * H), F32), extra], axis=1)

    b_second = first_ring.advance(b_second)
    own_second = own(x_second, second, wo_s, b_second, rows_second)
    own_second = first_ring.advance(own_second)
    push_second = dot_nt(b_second, rows_second).reshape(S, H, rows)
    push_second = first_ring.advance(push_second)
    first = first_ring.finish().reshape(R * n, 6 * H)
    b_first = jnp.where(slots < place, dot_tn(a_all, first[:, : 4 * H]), 0.0).astype(BF16)
    own_first = own(x_first, first, wo_f, b_first, rows_first)
    keep, away = ordered(own_first, own_second)

    push_first = dot_nt(b_first, rows_first).reshape(S, H, rows)
    push = (push_first + push_second[::-1]).astype(BF16)
    push, away = tied(push, away.astype(BF16))
    arrived = moved(away, "section", lambda i: i ^ 15)
    push = lax.all_to_all(push, "section", 0, 0)
    push = jnp.sum(push.astype(F32), axis=0).T
    out = keep + arrived.astype(F32)
    out = out + jnp.concatenate([jnp.zeros((rows, 3 * H), F32), push], axis=1)
    return out[None]


def solution(mesh):
    in_specs = (
        P("dp", None, None, None),
        P("dp", None, None),
        P("dp", None),
        P("section", None, None),
        P("section", None, None),
    )
    out_specs = P("section", "dp", None)
    return jax.shard_map(body, mesh=mesh, in_specs=in_specs, out_specs=out_specs, check_vma=False)
```
